512 devices in a mesh: tm: 256 (over z, y, x), seq: 2 (over core).
Axes of the slice: x: 4, y: 8, z: 8, core: 2. Of those that a mesh axis runs over, the one named last changes fastest.
Arguments:
- latents: float32 [256, 256, 64], P('tm', 'seq'), may hold values from -6 to 6
- timesteps: int32 [256], replicated, may hold values from 1 to 1024, as said below
- modulation: float32 [256, 5, 2048], P('tm'), may hold values from -4 to 4
- w_in: bfloat16 [64, 2048], replicated, may hold values from -0.25 to 0.25
- w_query: bfloat16 [2048, 2048], P(None, 'seq')
- w_key: bfloat16 [2048, 2048], P(None, 'seq')
- w_value: bfloat16 [2048, 2048], P(None, 'seq'), may hold values from -0.125 to 0.125
- w_attn_out: bfloat16 [2048, 2048], P('seq'), may hold values from -0.375 to 0.375
- w_final: bfloat16 [2048, 64], replicated, may hold values from -0.125 to 0.125
Outputs:
- next_latents: float32 [256, 256, 64], P('tm', 'seq')
The draws below stay inside these ranges and needn't reach their ends.
Inputs may be any that keep to these rules, and one draw needn't show every extreme that they name: `timesteps`: strictly decreasing; the first is 1024.
All inputs are finite; a program needn't handle non-finite values.
Results may differ from the reference program's by a relative error of at most 0.015.
Values may be sent and summed in bfloat16 or wider, within the bound.
No kernel may reach another device: no remote copies, remote signals or barrier semaphores. Data moves between devices by JAX's collectives and lax.ppermute only.
A program may use at most 128 MiB of HBM per device.

```python
import jax
import jax.numpy as jnp
from jax import lax

D = 2048
HEADS = 16
HEAD_DIM = 128
CH = 64
TSCALE = 1024
SEQ_TOK = 256
STEPS = 256
HEAD_GROUPS = 2
GROUP_HEADS = 8


def shared_query(key):
    return jax.random.normal(key, (D, HEADS * HEAD_DIM), jnp.float32) * D ** (-0.5)


def draw_w_query(key, part):
    shared_base = shared_query(key)
    return shared_base.astype(jnp.bfloat16)


def draw_w_key(key, part):
    key = jax.random.fold_in(key, 5)
    own_noise = jax.random.normal(key, (D, HEADS * HEAD_DIM), jnp.float32) * D ** (-0.5)
    return own_noise.astype(jnp.bfloat16)


def draw_timesteps(key, part):
    key = jax.random.fold_in(key, 11)
    stride = TSCALE // STEPS
    jitter = jax.random.randint(key, (STEPS,), 0, stride)
    position = jnp.arange(STEPS, dtype=jnp.int32)
    jitter = jnp.where(position == 0, 0, jitter)
    jitter = jnp.where(position == STEPS - 1, stride - 1, jitter)
    return ((STEPS - position) * stride - jitter).astype(jnp.int32)


def level_of(key, shape, split, low, high):
    def one(dim, parts):
        heights = jax.random.uniform(jax.random.fold_in(jax.random.fold_in(key, 6), dim), (parts,), jnp.float32, low / len(split), high / len(split))
        return jnp.repeat(jnp.exp(heights), shape[dim] // parts).reshape((-1,) + (1,) * (len(shape) - dim - 1))

    level = one(*split[0])
    for cut in split[1:]:
        level = level * one(*cut)
    return level


def centred(rng, shape, scale, reach, split=(), held_as=jnp.bfloat16):
    array = jax.random.normal(rng, shape, jnp.float32) * scale
    if len(split) > 0:
        array = level_of(rng, shape, split, -0.22, 0.18) * array
    return jnp.clip(array, min=-reach, max=reach).astype(held_as)


def setup_inputs(seed: int = 0) -> dict:
    arg_keys = jax.random.split(jax.random.key(seed), 10)
    latents = centred(arg_keys[0], (STEPS, SEQ_TOK, CH), 1.0, 6.0, ((0, 256), (1, 2)), jnp.float32)
    timesteps = draw_timesteps(jax.random.fold_in(arg_keys[9], 71), 0)
    modulation = centred(arg_keys[2], (STEPS, 5, D), 0.7, 4.0, ((0, 256),), jnp.float32)
    w_in = centred(arg_keys[3], (CH, D), 0.04, 0.25)
    w_query = draw_w_query(jax.random.fold_in(arg_keys[9], 71), 0)
    w_key = draw_w_key(jax.random.fold_in(arg_keys[9], 71), 0)
    w_value = centred(arg_keys[6], (D, HEADS * HEAD_DIM), D ** -0.5, 0.125, ((1, 2),))
    w_attn_out = centred(arg_keys[7], (HEADS * HEAD_DIM, D), (2 * HEAD_DIM) ** -0.5, 0.375, ((0, 2),))
    w_final = centred(arg_keys[8], (D, CH), D ** -0.5, 0.125)
    return {"latents": latents, "timesteps": timesteps, "modulation": modulation, "w_in": w_in, "w_query": w_query, "w_key": w_key, "w_value": w_value, "w_attn_out": w_attn_out, "w_final": w_final}


norm_eps = 1e-06

def layer_norm(values):
    center = values - lax.optimization_barrier(jnp.mean(values, axis=-1, keepdims=True))
    spread = lax.optimization_barrier(jnp.mean(center * center, axis=-1, keepdims=True))
    return center * lax.rsqrt(spread + norm_eps)

def rounded_part(product):
    narrow = lax.optimization_barrier(product.astype(jnp.bfloat16))
    return narrow.astype(jnp.float32)

def head_attention(queries, keys_all, values_all):
    scores = jnp.dot(queries, keys_all.T, preferred_element_type=jnp.float32) * HEAD_DIM ** (-0.5)
    row_peak = lax.optimization_barrier(jnp.max(scores, axis=-1, keepdims=True))
    weights = jnp.exp(scores - row_peak)
    weights = (weights / lax.optimization_barrier(jnp.sum(weights, axis=-1, keepdims=True))).astype(jnp.bfloat16)
    return jnp.dot(weights, values_all, preferred_element_type=jnp.float32).astype(jnp.bfloat16)

def drift_of(latent, modulate, w_in, w_query, w_key, w_value, w_attn_out, w_final):
    hidden = jnp.dot(latent.astype(jnp.bfloat16), w_in, preferred_element_type=jnp.float32)
    normed = (layer_norm(hidden) * (1.0 + modulate[1]) + modulate[0]).astype(jnp.bfloat16)
    queries = jnp.dot(normed, w_query, preferred_element_type=jnp.float32).astype(jnp.bfloat16)
    keys_all = jnp.dot(normed, w_key, preferred_element_type=jnp.float32).astype(jnp.bfloat16)
    values_all = jnp.dot(normed, w_value, preferred_element_type=jnp.float32).astype(jnp.bfloat16)

    def one_head(head_index):
        first_col = (head_index * HEAD_DIM).astype(jnp.int32)
        return head_attention(lax.dynamic_slice_in_dim(queries, first_col, HEAD_DIM, 1), lax.dynamic_slice_in_dim(keys_all, first_col, HEAD_DIM, 1), lax.dynamic_slice_in_dim(values_all, first_col, HEAD_DIM, 1))
    per_head = lax.map(one_head, jnp.arange(HEADS, dtype=jnp.int32))
    head_mixed = jnp.transpose(per_head, (1, 0, 2)).reshape(SEQ_TOK, HEADS * HEAD_DIM)
    group_cols = GROUP_HEADS * HEAD_DIM
    attended = jnp.zeros((SEQ_TOK, D), jnp.float32)
    for group_index in range(HEAD_GROUPS):
        low = group_index * group_cols
        product = jnp.dot(head_mixed[:, low:low + group_cols], w_attn_out[low:low + group_cols], preferred_element_type=jnp.float32)
        attended = attended + rounded_part(product)
    resid = hidden + modulate[2] * attended
    final = (layer_norm(resid) * (1.0 + modulate[4]) + modulate[3]).astype(jnp.bfloat16)
    return jnp.dot(final, w_final, preferred_element_type=jnp.float32)

def reference(latents, timesteps, modulation, w_in, w_query, w_key, w_value, w_attn_out, w_final):

    def step_drift(step_index):
        return drift_of(latents[step_index], modulation[step_index], w_in, w_query, w_key, w_value, w_attn_out, w_final)
    drifts = lax.map(step_drift, jnp.arange(STEPS, dtype=jnp.int32))
    time_values = timesteps.astype(jnp.float32)
    following = jnp.concatenate([time_values[1:], jnp.zeros((1,), jnp.float32)])
    step_sizes = (following - time_values) / TSCALE
    step_terms = step_sizes[:, None, None] * drifts
    return jnp.cumsum(step_terms, axis=0)
```

```python
import jax
import jax.numpy as jnp
from jax import lax
from jax.sharding import PartitionSpec as P

HEAD_DIM = 128
TSCALE = 1024
STAGES = (4, 8, 8)

norm_eps = 1e-06


def layer_norm(values):
    center = values - jnp.mean(values, axis=-1, keepdims=True)
    spread = jnp.mean(center * center, axis=-1, keepdims=True)
    return center * lax.rsqrt(spread + norm_eps)


def modulated(hidden, modulate):
    return (layer_norm(hidden) * (1.0 + modulate[1]) + modulate[0]).astype(jnp.bfloat16)


def attend_heads(queries, keys_all, values_all):
    token_count = queries.shape[0]
    local_heads = queries.shape[1] // HEAD_DIM
    queries = queries.reshape(token_count, local_heads, HEAD_DIM)
    keys_heads = keys_all.reshape(token_count, local_heads, HEAD_DIM)
    values_heads = values_all.reshape(token_count, local_heads, HEAD_DIM)
    scores = jnp.einsum(
        "qhd,khd->hqk", queries, keys_heads, preferred_element_type=jnp.float32
    ) * HEAD_DIM ** (-0.5)
    row_peak = jnp.max(scores, axis=-1, keepdims=True)
    weights = jnp.exp(scores - row_peak)
    weights = (weights / jnp.sum(weights, axis=-1, keepdims=True)).astype(jnp.bfloat16)
    mixed = jnp.einsum(
        "hqk,khd->qhd", weights, values_heads, preferred_element_type=jnp.float32
    ).astype(jnp.bfloat16)
    return mixed.reshape(token_count, local_heads * HEAD_DIM)


def along(stage, count):
    below = 1
    for size in STAGES[:stage]:
        below *= size
    size = STAGES[stage]
    return [
        [outer * below * size + place * below + inner for place in range(size)]
        for outer in range(count // (below * size))
        for inner in range(below)
    ]


def prefix_over_steps(term):
    count = lax.axis_size("tm")
    place = lax.axis_index("tm")
    prefix = term
    total = term
    for stage, size in enumerate(STAGES):
        here = place % size
        place = place // size
        block = jnp.broadcast_to(total.astype(jnp.bfloat16)[None], (size,) + total.shape)
        parts = lax.all_to_all(
            block, "tm", 0, 0, axis_index_groups=along(stage, count)
        ).astype(jnp.float32)
        earlier = (jnp.arange(size, dtype=jnp.int32) < here)[:, None, None]
        prefix = prefix + jnp.sum(jnp.where(earlier, parts, 0.0), axis=0)
        total = jnp.sum(parts, axis=0)
    return prefix


def on_device(latents, timesteps, modulation, w_in, w_query, w_key, w_value, w_attn_out, w_final):
    swap = [(0, 1), (1, 0)]
    own_latent = latents[0].T
    other_latent = lax.ppermute(own_latent, "seq", swap)
    modulate = modulation[0]

    def hidden_of(latent):
        return lax.dot_general(
            latent.astype(jnp.bfloat16), w_in, (((0,), (0,)), ((), ())), preferred_element_type=jnp.float32
        )

    own_hidden = hidden_of(own_latent)
    normed = jnp.concatenate(
        [modulated(own_hidden, modulate), modulated(hidden_of(other_latent), modulate)]
    )

    def project(weight):
        return jnp.dot(normed, weight, preferred_element_type=jnp.float32).astype(jnp.bfloat16)

    head_mixed = attend_heads(project(w_query), project(w_key), project(w_value))
    partial = jnp.dot(head_mixed, w_attn_out, preferred_element_type=jnp.float32).astype(jnp.bfloat16)
    token_count = own_hidden.shape[0]
    received = lax.ppermute(partial[token_count:], "seq", swap)
    attended = partial[:token_count].astype(jnp.float32) + received.astype(jnp.float32)
    resid = own_hidden + modulate[2] * attended
    final = (layer_norm(resid) * (1.0 + modulate[4]) + modulate[3]).astype(jnp.bfloat16)
    drift = lax.dot_general(
        w_final, final, (((0,), (1,)), ((), ())), preferred_element_type=jnp.float32
    )
    step_index = lax.axis_index("tm")
    step_count = lax.axis_size("tm")
    time_values = timesteps.astype(jnp.float32)
    current = time_values[step_index]
    following = jnp.where(
        step_index + 1 < step_count, time_values[jnp.minimum(step_index + 1, step_count - 1)], 0.0
    )
    step_size = (following - current) / TSCALE
    return prefix_over_steps(step_size * drift).T[None]


def solution(mesh):
    placed = (
        P("tm", "seq", None),
        P(),
        P("tm", None, None),
        P(),
        P(None, "seq"),
        P(None, "seq"),
        P(None, "seq"),
        P("seq", None),
        P(),
    )
    return jax.shard_map(
        on_device, mesh=mesh, in_specs=placed, out_specs=P("tm", "seq", None), check_vma=False
    )
```

```python
import jax
import jax.numpy as jnp
from jax import lax
from jax.sharding import PartitionSpec as P

HEAD_DIM = 128
TSCALE = 1024
NX, NY, NZ = 4, 8, 8

norm_eps = 1e-06


def layer_norm(values):
    center = values - jnp.mean(values, axis=-1, keepdims=True)
    spread = jnp.mean(center * center, axis=-1, keepdims=True)
    return center * lax.rsqrt(spread + norm_eps)


def modulated(hidden, modulate):
    return (layer_norm(hidden) * (1.0 + modulate[1]) + modulate[0]).astype(jnp.bfloat16)


def attend_heads(queries, keys_all, values_all):
    token_count = queries.shape[0]
    local_heads = queries.shape[1] // HEAD_DIM
    queries = queries.reshape(token_count, local_heads, HEAD_DIM)
    keys_heads = keys_all.reshape(token_count, local_heads, HEAD_DIM)
    values_heads = values_all.reshape(token_count, local_heads, HEAD_DIM)
    scores = jnp.einsum(
        "qhd,khd->hqk", queries, keys_heads, preferred_element_type=jnp.float32
    ) * HEAD_DIM ** (-0.5)
    row_peak = jnp.max(scores, axis=-1, keepdims=True)
    weights = jnp.exp(scores - row_peak)
    weights = (weights / jnp.sum(weights, axis=-1, keepdims=True)).astype(jnp.bfloat16)
    mixed = jnp.einsum(
        "hqk,khd->qhd", weights, values_heads, preferred_element_type=jnp.float32
    ).astype(jnp.bfloat16)
    return mixed.reshape(token_count, local_heads * HEAD_DIM)


def same(count, key):
    groups = {}
    for step in range(count):
        groups.setdefault(key(*place_of(step)), []).append(step)
    return list(groups.values())


def place_of(step):
    return step % NX, step // NX % NY, step // (NX * NY)


def step_of(x, y, z):
    return (z * NY + y) * NX + x


def prefix_over_steps(term):
    count = lax.axis_size("tm")
    x, y, z = place_of(lax.axis_index("tm"))
    near = jnp.arange(4 * NX, dtype=jnp.int32)
    far = jnp.arange(NY * NZ // 4, dtype=jnp.int32)
    member = step_of(near % NX, y // 2 * 2 + near // NX % 2, z // 2 * 2 + near // (2 * NX))
    target = step_of(x, far % (NY // 2) * 2 + y % 2, far // (NY // 2) * 2 + z % 2)
    wanted = (member[None, :] <= target[:, None]).astype(jnp.bfloat16)
    block = jnp.broadcast_to(term.astype(jnp.bfloat16)[None], near.shape + term.shape)
    block, wanted = lax.optimization_barrier((block, wanted))
    gathered = lax.all_to_all(
        block, "tm", 0, 0, axis_index_groups=same(count, lambda x, y, z: (y // 2, z // 2))
    )
    sums = lax.dot_general(
        wanted, gathered, (((1,), (0,)), ((), ())), preferred_element_type=jnp.float32
    ).astype(jnp.bfloat16)
    parts = lax.all_to_all(
        sums, "tm", 0, 0, axis_index_groups=same(count, lambda x, y, z: (x, y % 2, z % 2))
    )
    return jnp.sum(parts.astype(jnp.float32), axis=0)


def on_device(latents, timesteps, modulation, w_in, w_query, w_key, w_value, w_attn_out, w_final):
    swap = [(0, 1), (1, 0)]
    own_latent = latents[0].T
    other_latent = lax.ppermute(own_latent, "seq", swap)
    modulate = modulation[0]

    def hidden_of(latent):
        return lax.dot_general(
            latent.astype(jnp.bfloat16), w_in, (((0,), (0,)), ((), ())), preferred_element_type=jnp.float32
        )

    own_hidden = hidden_of(own_latent)
    normed = jnp.concatenate(
        [modulated(own_hidden, modulate), modulated(hidden_of(other_latent), modulate)]
    )

    def project(weight):
        return jnp.dot(normed, weight, preferred_element_type=jnp.float32).astype(jnp.bfloat16)

    head_mixed = attend_heads(project(w_query), project(w_key), project(w_value))
    partial = jnp.dot(head_mixed, w_attn_out, preferred_element_type=jnp.float32).astype(jnp.bfloat16)
    token_count = own_hidden.shape[0]
    received = lax.ppermute(partial[token_count:], "seq", swap)
    attended = partial[:token_count].astype(jnp.float32) + received.astype(jnp.float32)
    resid = own_hidden + modulate[2] * attended
    final = (layer_norm(resid) * (1.0 + modulate[4]) + modulate[3]).astype(jnp.bfloat16)
    drift = lax.dot_general(
        w_final, final, (((0,), (1,)), ((), ())), preferred_element_type=jnp.float32
    )
    step_index = lax.axis_index("tm")
    step_count = lax.axis_size("tm")
    time_values = timesteps.astype(jnp.float32)
    current = time_values[step_index]
    following = jnp.where(
        step_index + 1 < step_count, time_values[jnp.minimum(step_index + 1, step_count - 1)], 0.0
    )
    step_size = (following - current) / TSCALE
    return prefix_over_steps(step_size * drift).T[None]


def solution(mesh):
    placed = (
        P("tm", "seq", None),
        P(),
        P("tm", None, None),
        P(),
        P(None, "seq"),
        P(None, "seq"),
        P(None, "seq"),
        P("seq", None),
        P(),
    )
    return jax.shard_map(
        on_device, mesh=mesh, in_specs=placed, out_specs=P("tm", "seq", None), check_vma=False
    )
```

```python
import jax
import jax.numpy as jnp
from jax import lax
from jax.experimental import pallas as pl
from jax.experimental.pallas import tpu as pltpu
from jax.sharding import PartitionSpec as P

HEAD_DIM = 128
PAIR = 2 * HEAD_DIM
LOG2_E = 1.4426950408889634
AHEAD = 5
SKEW = True
TSCALE = 1024
NX, NY, NZ = 4, 8, 8

norm_eps = 1e-06


def layer_norm(values):
    center = values - jnp.mean(values, axis=-1, keepdims=True)
    spread = jnp.mean(center * center, axis=-1, keepdims=True)
    return center * lax.rsqrt(spread + norm_eps)


def hidden_of(latent, w_in):
    return lax.dot_general(
        latent.astype(jnp.bfloat16), w_in, (((0,), (0,)), ((), ())), preferred_element_type=jnp.float32
    )


def attention_kernel(
    other_latent, own_latent, modulate, w_in, w_query, w_key, w_value, w_attn_out,
    keep, send, latent, modulate_held, w_in_held, normed, mixed, w_held, w_out_held, small_sems, sems,
):
    half = own_latent.shape[1]
    small = [
        pltpu.make_async_copy(own_latent, latent.at[0], small_sems.at[0]),
        pltpu.make_async_copy(other_latent, latent.at[1], small_sems.at[1]),
        pltpu.make_async_copy(w_in, w_in_held, small_sems.at[2]),
        pltpu.make_async_copy(modulate, modulate_held, small_sems.at[3]),
    ]
    queue = []
    for block in range(w_held.shape[0]):
        for which, weight in enumerate((w_query, w_key, w_value)):
            queue.append((weight.at[:, pl.ds(block * PAIR, PAIR)], w_held.at[block, which]))
    for first in range(0, w_attn_out.shape[0], PAIR):
        rows = pl.ds(first, PAIR)
        queue.append((w_attn_out.at[rows, :], w_out_held.at[rows, :]))
    queue = [pltpu.make_async_copy(*ends, sems.at[i]) for i, ends in enumerate(queue)]
    waited = []

    def arrive():
        queue[len(waited)].wait()
        if len(waited) + AHEAD < len(queue):
            queue[len(waited) + AHEAD].start()
        waited.append(True)

    for copy in small + queue[:AHEAD]:
        copy.start()
    for copy in small:
        copy.wait()

    for place in range(2):
        hidden = hidden_of(latent[place], w_in_held[...])
        shaped = layer_norm(hidden) * (1.0 + modulate_held[1]) + modulate_held[0]
        normed[place * half : (place + 1) * half, :] = shaped.astype(jnp.bfloat16)

    def project(block, which):
        return jnp.dot(
            normed[...], w_held[block, which], preferred_element_type=jnp.float32
        ).astype(jnp.bfloat16)

    ones = jnp.ones((2 * half, HEAD_DIM), jnp.bfloat16)

    def attend(block, query, key, value):
        for head in range(PAIR // HEAD_DIM):
            cols = slice(head * HEAD_DIM, (head + 1) * HEAD_DIM)
            scores = lax.dot_general(
                query[:, cols], key[:, cols], (((1,), (1,)), ((), ())), preferred_element_type=jnp.float32
            )
            peak = jnp.max(scores, axis=-1, keepdims=True)
            weights = jnp.exp2((scores - peak) * (HEAD_DIM ** (-0.5) * LOG2_E)).astype(jnp.bfloat16)
            both = jnp.dot(
                weights,
                jnp.concatenate([value[:, cols], ones], axis=1),
                preferred_element_type=jnp.float32,
            )
            first = block * PAIR + head * HEAD_DIM
            mixed[:, first : first + HEAD_DIM] = (both[:, :HEAD_DIM] / both[:, HEAD_DIM:]).astype(
                jnp.bfloat16
            )

    before = None
    for block in range(w_held.shape[0]):
        for which in range(3):
            arrive()
        projected = [project(block, which) for which in range(3)]
        if SKEW:
            if before is not None:
                attend(block - 1, *before)
            before = projected
        else:
            attend(block, *projected)
    if SKEW:
        attend(block, *before)
    while len(waited) < len(queue):
        arrive()
    for first in range(0, keep.shape[1], PAIR):
        cols = slice(first, first + PAIR)
        partial = jnp.dot(
            mixed[...], w_out_held[:, cols], preferred_element_type=jnp.float32
        ).astype(jnp.bfloat16)
        keep[:, cols] = partial[:half]
        send[:, cols] = partial[half:]


def attention(other_latent, own_latent, modulate, w_in, w_query, w_key, w_value, w_attn_out):
    half = own_latent.shape[1]
    width, cols = w_query.shape
    blocks = cols // PAIR
    part = jax.ShapeDtypeStruct((half, width), jnp.bfloat16)
    return pl.pallas_call(
        attention_kernel,
        out_shape=(part, part),
        in_specs=[pl.BlockSpec(memory_space=pl.ANY)] * 8,
        out_specs=(pl.BlockSpec(memory_space=pltpu.VMEM),) * 2,
        scratch_shapes=[
            pltpu.VMEM((2,) + own_latent.shape, jnp.float32),
            pltpu.VMEM(modulate.shape, jnp.float32),
            pltpu.VMEM(w_in.shape, jnp.bfloat16),
            pltpu.VMEM((2 * half, width), jnp.bfloat16),
            pltpu.VMEM((2 * half, cols), jnp.bfloat16),
            pltpu.VMEM((blocks, 3, width, PAIR), jnp.bfloat16),
            pltpu.VMEM(w_attn_out.shape, jnp.bfloat16),
            pltpu.SemaphoreType.DMA((4,)),
            pltpu.SemaphoreType.DMA((4 * blocks,)),
        ],
        compiler_params=pltpu.CompilerParams(vmem_limit_bytes=36 * 2**20),
        cost_estimate=pl.CostEstimate(
            flops=2 * 2 * half * width * cols * 4, bytes_accessed=2 * width * cols * 4, transcendentals=0
        ),
    )(other_latent, own_latent, modulate, w_in, w_query, w_key, w_value, w_attn_out)


def same(count, key):
    groups = {}
    for step in range(count):
        groups.setdefault(key(*place_of(step)), []).append(step)
    return list(groups.values())


def place_of(step):
    return step % NX, step // NX % NY, step // (NX * NY)


def step_of(x, y, z):
    return (z * NY + y) * NX + x


def prefix_over_steps(term):
    count = lax.axis_size("tm")
    x, y, z = place_of(lax.axis_index("tm"))
    near = jnp.arange(4 * NX, dtype=jnp.int32)
    far = jnp.arange(NY * NZ // 4, dtype=jnp.int32)
    member = step_of(near % NX, y // 2 * 2 + near // NX % 2, z // 2 * 2 + near // (2 * NX))
    target = step_of(x, far % (NY // 2) * 2 + y % 2, far // (NY // 2) * 2 + z % 2)
    wanted = (member[None, :] <= target[:, None]).astype(jnp.bfloat16)
    block = jnp.broadcast_to(term.astype(jnp.bfloat16)[None], near.shape + term.shape)
    block, wanted = lax.optimization_barrier((block, wanted))
    gathered = lax.all_to_all(
        block, "tm", 0, 0, axis_index_groups=same(count, lambda x, y, z: (y // 2, z // 2))
    )
    sums = lax.dot_general(
        wanted, gathered, (((1,), (0,)), ((), ())), preferred_element_type=jnp.float32
    ).astype(jnp.bfloat16)
    parts = lax.all_to_all(
        sums, "tm", 0, 0, axis_index_groups=same(count, lambda x, y, z: (x, y % 2, z % 2))
    )
    return jnp.sum(parts.astype(jnp.float32), axis=0)


def on_device(latents, timesteps, modulation, w_in, w_query, w_key, w_value, w_attn_out, w_final):
    swap = [(0, 1), (1, 0)]
    own_latent = latents[0].T
    other_latent = lax.ppermute(own_latent, "seq", swap)
    modulate = jnp.transpose(modulation, (1, 0, 2))
    there = [
        pltpu.with_memory_space_constraint(array, pltpu.HBM)
        for array in (own_latent, modulate, w_in, w_query, w_key, w_value, w_attn_out)
    ]
    keep, send = attention(other_latent, *there)
    received = lax.ppermute(send, "seq", swap)
    own_latent, keep = lax.optimization_barrier((own_latent, keep))
    hidden = hidden_of(own_latent, w_in)
    attended = keep.astype(jnp.float32) + received.astype(jnp.float32)
    resid = hidden + modulate[2] * attended
    final = (layer_norm(resid) * (1.0 + modulate[4]) + modulate[3]).astype(jnp.bfloat16)
    drift = lax.dot_general(
        w_final, final, (((0,), (1,)), ((), ())), preferred_element_type=jnp.float32
    )
    step_index = lax.axis_index("tm")
    step_count = lax.axis_size("tm")
    time_values = timesteps.astype(jnp.float32)
    current = time_values[step_index]
    following = jnp.where(
        step_index + 1 < step_count, time_values[jnp.minimum(step_index + 1, step_count - 1)], 0.0
    )
    step_size = (following - current) / TSCALE
    return prefix_over_steps(step_size * drift).T[None]


def solution(mesh):
    placed = (
        P("tm", "seq", None),
        P(),
        P("tm", None, None),
        P(),
        P(None, "seq"),
        P(None, "seq"),
        P(None, "seq"),
        P("seq", None),
        P(),
    )
    return jax.shard_map(
        on_device, mesh=mesh, in_specs=placed, out_specs=P("tm", "seq", None), check_vma=False
    )
```

```python
import jax
import jax.numpy as jnp
from jax import lax
from jax.experimental import pallas as pl
from jax.experimental.pallas import tpu as pltpu
from jax.sharding import PartitionSpec as P

HEAD_DIM = 128
PAIR = 2 * HEAD_DIM
LOG2_E = 1.4426950408889634
AHEAD = 5
TSCALE = 1024
NX, NY, NZ = 4, 8, 8

norm_eps = 1e-06


def layer_norm(values):
    center = values - jnp.mean(values, axis=-1, keepdims=True)
    spread = jnp.mean(center * center, axis=-1, keepdims=True)
    return center * lax.rsqrt(spread + norm_eps)


def hidden_of(latent, w_in):
    return lax.dot_general(
        latent.astype(jnp.bfloat16), w_in, (((0,), (0,)), ((), ())), preferred_element_type=jnp.float32
    )


def shaped(hidden, gain, shift):
    return (layer_norm(hidden) * gain + shift).astype(jnp.bfloat16)


def front_kernel(
    own_latent, modulate, w_in, timesteps, w_query, w_key, w_value,
    normed, first, w_in_held, modulate_held, latent, timesteps_held, small_sems, sems,
):
    small = [
        pltpu.make_async_copy(own_latent, latent, small_sems.at[0]),
        pltpu.make_async_copy(w_in, w_in_held, small_sems.at[1]),
        pltpu.make_async_copy(modulate, modulate_held, small_sems.at[2]),
        pltpu.make_async_copy(timesteps, timesteps_held, small_sems.at[3]),
    ]
    weights = [
        pltpu.make_async_copy(
            weight.at[:, pl.ds(0, PAIR)], first.at[which], sems.at[which]
        )
        for which, weight in enumerate((w_query, w_key, w_value))
    ]
    for copy in small + weights:
        copy.start()
    for copy in small:
        copy.wait()
    normed[...] = shaped(hidden_of(latent[...], w_in_held[...]), 1.0 + modulate_held[1], modulate_held[0])
    for copy in weights:
        copy.wait()


def front(own_latent, modulate, w_in, timesteps, w_query, w_key, w_value):
    half = own_latent.shape[1]
    width = w_in.shape[1]
    return pl.pallas_call(
        front_kernel,
        out_shape=(
            jax.ShapeDtypeStruct((half, width), jnp.bfloat16),
            jax.ShapeDtypeStruct((3, width, PAIR), jnp.bfloat16),
            jax.ShapeDtypeStruct(w_in.shape, jnp.bfloat16),
            jax.ShapeDtypeStruct(modulate.shape, jnp.float32),
            jax.ShapeDtypeStruct(own_latent.shape, jnp.float32),
            jax.ShapeDtypeStruct(timesteps.shape, jnp.int32),
        ),
        in_specs=[pl.BlockSpec(memory_space=pl.ANY)] * 7,
        out_specs=(pl.BlockSpec(memory_space=pltpu.VMEM),) * 6,
        scratch_shapes=[
            pltpu.SemaphoreType.DMA((4,)),
            pltpu.SemaphoreType.DMA((3,)),
        ],
        compiler_params=pltpu.CompilerParams(vmem_limit_bytes=24 * 2**20),
        cost_estimate=pl.CostEstimate(
            flops=2 * half * width * w_in.shape[0], bytes_accessed=6 * width * PAIR, transcendentals=0
        ),
    )(own_latent, modulate, w_in, timesteps, w_query, w_key, w_value)


def attention_kernel(
    other_latent, own_normed, first, w_in, modulate, w_query, w_key, w_value, w_attn_out,
    send, own_mixed, w_out_held, normed, mixed, w_held, sems,
):
    half = other_latent.shape[1]
    blocks = 1 + w_held.shape[0]
    queue = []
    for block in range(1, blocks):
        for which, weight in enumerate((w_query, w_key, w_value)):
            queue.append((weight.at[:, pl.ds(block * PAIR, PAIR)], w_held.at[block - 1, which]))
    for row in range(0, w_attn_out.shape[0], PAIR):
        rows = pl.ds(row, PAIR)
        queue.append((w_attn_out.at[rows, :], w_out_held.at[rows, :]))
    queue = [pltpu.make_async_copy(*ends, sems.at[i]) for i, ends in enumerate(queue)]
    waited = []

    def arrive():
        queue[len(waited)].wait()
        if len(waited) + AHEAD < len(queue):
            queue[len(waited) + AHEAD].start()
        waited.append(True)

    for copy in queue[:AHEAD]:
        copy.start()

    normed[:half, :] = own_normed[...]
    normed[half:, :] = shaped(hidden_of(other_latent[...], w_in[...]), 1.0 + modulate[1], modulate[0])

    def project(block, which):
        weight = first[which] if block == 0 else w_held[block - 1, which]
        return jnp.dot(normed[...], weight, preferred_element_type=jnp.float32).astype(jnp.bfloat16)

    ones = jnp.ones((2 * half, HEAD_DIM), jnp.bfloat16)

    def attend(block, query, key, value):
        for head in range(PAIR // HEAD_DIM):
            cols = slice(head * HEAD_DIM, (head + 1) * HEAD_DIM)
            scores = lax.dot_general(
                query[:, cols], key[:, cols], (((1,), (1,)), ((), ())), preferred_element_type=jnp.float32
            )
            peak = jnp.max(scores, axis=-1, keepdims=True)
            weights = jnp.exp2((scores - peak) * (HEAD_DIM ** (-0.5) * LOG2_E)).astype(jnp.bfloat16)
            both = jnp.dot(
                weights,
                jnp.concatenate([value[:, cols], ones], axis=1),
                preferred_element_type=jnp.float32,
            )
            result = (both[:, :HEAD_DIM] / both[:, HEAD_DIM:]).astype(jnp.bfloat16)
            col = block * PAIR + head * HEAD_DIM
            own_mixed[:, col : col + HEAD_DIM] = result[:half]
            mixed[:, col : col + HEAD_DIM] = result[half:]

    before = [project(0, which) for which in range(3)]
    for block in range(1, blocks):
        for which in range(3):
            arrive()
        projected = [project(block, which) for which in range(3)]
        attend(block - 1, *before)
        before = projected
    attend(blocks - 1, *before)
    while len(waited) < len(queue):
        arrive()
    for col in range(0, send.shape[1], PAIR):
        cols = slice(col, col + PAIR)
        send[:, cols] = jnp.dot(
            mixed[...], w_out_held[:, cols], preferred_element_type=jnp.float32
        ).astype(jnp.bfloat16)


def attention(other_latent, own_normed, first, w_in, modulate, w_query, w_key, w_value, w_attn_out):
    half = other_latent.shape[1]
    width, cols = w_query.shape
    blocks = cols // PAIR
    return pl.pallas_call(
        attention_kernel,
        out_shape=(
            jax.ShapeDtypeStruct((half, width), jnp.bfloat16),
            jax.ShapeDtypeStruct((half, cols), jnp.bfloat16),
            jax.ShapeDtypeStruct(w_attn_out.shape, jnp.bfloat16),
        ),
        in_specs=[pl.BlockSpec(memory_space=pltpu.VMEM)] * 5 + [pl.BlockSpec(memory_space=pl.ANY)] * 4,
        out_specs=(pl.BlockSpec(memory_space=pltpu.VMEM),) * 3,
        scratch_shapes=[
            pltpu.VMEM((2 * half, width), jnp.bfloat16),
            pltpu.VMEM((half, cols), jnp.bfloat16),
            pltpu.VMEM((blocks - 1, 3, width, PAIR), jnp.bfloat16),
            pltpu.SemaphoreType.DMA((4 * blocks - 3,)),
        ],
        compiler_params=pltpu.CompilerParams(vmem_limit_bytes=32 * 2**20),
        cost_estimate=pl.CostEstimate(
            flops=2 * 2 * half * width * cols * 4, bytes_accessed=2 * width * cols * 4, transcendentals=0
        ),
    )(other_latent, own_normed, first, w_in, modulate, w_query, w_key, w_value, w_attn_out)


def own_rows_kernel(own_latent, w_in, modulate, timesteps, chosen, own_mixed, w_attn_out, out, step_size):
    times = jnp.sum(timesteps[...].astype(jnp.float32) * chosen[...], axis=1, keepdims=True)
    step_size[...] = jnp.broadcast_to((times[1:] - times[:1]) / TSCALE, step_size.shape)
    for col in range(0, out.shape[1], PAIR):
        cols = slice(col, col + PAIR)
        partial = jnp.dot(
            own_mixed[...], w_attn_out[:, cols], preferred_element_type=jnp.float32
        ).astype(jnp.bfloat16)
        out[:, cols] = hidden_of(own_latent[...], w_in[:, cols]) + modulate[2, :, cols] * partial.astype(
            jnp.float32
        )


def own_rows(own_latent, w_in, modulate, timesteps, chosen, own_mixed, w_attn_out):
    half, cols = own_mixed.shape
    width = w_attn_out.shape[1]
    return pl.pallas_call(
        own_rows_kernel,
        out_shape=(
            jax.ShapeDtypeStruct((half, width), jnp.float32),
            jax.ShapeDtypeStruct((1, half), jnp.float32),
        ),
        in_specs=[pl.BlockSpec(memory_space=pltpu.VMEM)] * 7,
        out_specs=(pl.BlockSpec(memory_space=pltpu.VMEM),) * 2,
        compiler_params=pltpu.CompilerParams(vmem_limit_bytes=24 * 2**20),
        cost_estimate=pl.CostEstimate(
            flops=2 * half * width * cols, bytes_accessed=4 * half * width, transcendentals=0
        ),
    )(own_latent, w_in, modulate, timesteps, chosen, own_mixed, w_attn_out)


def same(count, key):
    groups = {}
    for step in range(count):
        groups.setdefault(key(*place_of(step)), []).append(step)
    return list(groups.values())


def place_of(step):
    return step % NX, step // NX % NY, step // (NX * NY)


def step_of(x, y, z):
    return (z * NY + y) * NX + x


def prefix_over_steps(term):
    count = lax.axis_size("tm")
    x, y, z = place_of(lax.axis_index("tm"))
    near = jnp.arange(4 * NX, dtype=jnp.int32)
    far = jnp.arange(NY * NZ // 4, dtype=jnp.int32)
    member = step_of(near % NX, y // 2 * 2 + near // NX % 2, z // 2 * 2 + near // (2 * NX))
    target = step_of(x, far % (NY // 2) * 2 + y % 2, far // (NY // 2) * 2 + z % 2)
    wanted = (member[None, :] <= target[:, None]).astype(jnp.bfloat16)
    block = jnp.broadcast_to(term.astype(jnp.bfloat16)[None], near.shape + term.shape)
    block, wanted = lax.optimization_barrier((block, wanted))
    gathered = lax.all_to_all(
        block, "tm", 0, 0, axis_index_groups=same(count, lambda x, y, z: (y // 2, z // 2))
    )
    sums = lax.dot_general(
        wanted, gathered, (((1,), (0,)), ((), ())), preferred_element_type=jnp.float32
    ).astype(jnp.bfloat16)
    parts = lax.all_to_all(
        sums, "tm", 0, 0, axis_index_groups=same(count, lambda x, y, z: (x, y % 2, z % 2))
    )
    return jnp.sum(parts.astype(jnp.float32), axis=0)


def on_device(latents, timesteps, modulation, w_in, w_query, w_key, w_value, w_attn_out, w_final):
    swap = [(0, 1), (1, 0)]
    own_latent = latents[0].T
    other_latent = lax.ppermute(own_latent, "seq", swap)
    modulate = jnp.transpose(modulation, (1, 0, 2))
    there = [
        pltpu.with_memory_space_constraint(array, pltpu.HBM)
        for array in (own_latent, modulate, w_in, timesteps[None], w_query, w_key, w_value, w_attn_out)
    ]
    own_normed, first, w_in_held, modulate, own_latent, times = front(*there[:7])
    send, own_mixed, w_out_held = attention(
        other_latent, own_normed, first, w_in_held, modulate, *there[4:]
    )
    received = lax.ppermute(send, "seq", swap)
    ahead = jnp.arange(timesteps.shape[0], dtype=jnp.int32)[None] - lax.axis_index("tm")
    chosen = (ahead == jnp.arange(2, dtype=jnp.int32)[:, None]).astype(jnp.float32)
    own_part, step_size = own_rows(
        own_latent, w_in_held, modulate, times, chosen, own_mixed, w_out_held
    )
    resid = own_part + modulate[2] * received.astype(jnp.float32)
    final = (layer_norm(resid) * (1.0 + modulate[4]) + modulate[3]).astype(jnp.bfloat16)
    drift = lax.dot_general(
        w_final, final, (((0,), (1,)), ((), ())), preferred_element_type=jnp.float32
    )
    return prefix_over_steps(step_size * drift).T[None]


def solution(mesh):
    placed = (
        P("tm", "seq", None),
        P(),
        P("tm", None, None),
        P(),
        P(None, "seq"),
        P(None, "seq"),
        P(None, "seq"),
        P("seq", None),
        P(),
    )
    return jax.shard_map(
        on_device, mesh=mesh, in_specs=placed, out_specs=P("tm", "seq", None), check_vma=False
    )
```

```python
import jax
import jax.numpy as jnp
from jax import lax
from jax.experimental import pallas as pl
from jax.experimental.pallas import tpu as pltpu
from jax.sharding import PartitionSpec as P

HEAD_DIM = 128
PAIR = 2 * HEAD_DIM
LOG2_E = 1.4426950408889634
TSCALE = 1024
NX, NY, NZ = 4, 8, 8

norm_eps = 1e-06


def layer_norm(values):
    center = values - jnp.mean(values, axis=-1, keepdims=True)
    spread = jnp.mean(center * center, axis=-1, keepdims=True)
    return center * lax.rsqrt(spread + norm_eps)


def hidden_of(latent, w_in):
    return lax.dot_general(
        latent.astype(jnp.bfloat16), w_in, (((0,), (0,)), ((), ())), preferred_element_type=jnp.float32
    )


def shaped(hidden, gain, shift):
    return (layer_norm(hidden) * gain + shift).astype(jnp.bfloat16)


def front_kernel(
    own_latent, modulate, w_in, timesteps, w_query, w_key,
    normed, first, w_in_held, modulate_held, latent, timesteps_held, small_sems, sems,
):
    small = [
        pltpu.make_async_copy(own_latent, latent, small_sems.at[0]),
        pltpu.make_async_copy(w_in, w_in_held, small_sems.at[1]),
        pltpu.make_async_copy(modulate, modulate_held, small_sems.at[2]),
        pltpu.make_async_copy(timesteps, timesteps_held, small_sems.at[3]),
    ]
    weights = [
        pltpu.make_async_copy(
            weight.at[:, pl.ds(0, PAIR)], first.at[which], sems.at[which]
        )
        for which, weight in enumerate((w_query, w_key))
    ]
    for copy in small:
        copy.start()
    for copy in weights:
        copy.start(priority=1)
    for copy in small:
        copy.wait()
    normed[...] = shaped(hidden_of(latent[...], w_in_held[...]), 1.0 + modulate_held[1], modulate_held[0])
    for copy in weights:
        copy.wait()


def front(own_latent, modulate, w_in, timesteps, w_query, w_key):
    half = own_latent.shape[1]
    width = w_in.shape[1]
    return pl.pallas_call(
        front_kernel,
        out_shape=(
            jax.ShapeDtypeStruct((half, width), jnp.bfloat16),
            jax.ShapeDtypeStruct((2, width, PAIR), jnp.bfloat16),
            jax.ShapeDtypeStruct(w_in.shape, jnp.bfloat16),
            jax.ShapeDtypeStruct(modulate.shape, jnp.float32),
            jax.ShapeDtypeStruct(own_latent.shape, jnp.float32),
            jax.ShapeDtypeStruct(timesteps.shape, jnp.int32),
        ),
        in_specs=[pl.BlockSpec(memory_space=pl.ANY)] * 6,
        out_specs=(pl.BlockSpec(memory_space=pltpu.VMEM),) * 6,
        scratch_shapes=[
            pltpu.SemaphoreType.DMA((4,)),
            pltpu.SemaphoreType.DMA((2,)),
        ],
        compiler_params=pltpu.CompilerParams(vmem_limit_bytes=24 * 2**20),
        cost_estimate=pl.CostEstimate(
            flops=2 * half * width * w_in.shape[0], bytes_accessed=6 * width * PAIR, transcendentals=0
        ),
    )(own_latent, modulate, w_in, timesteps, w_query, w_key)


def norm_kernel(other_latent, own_normed, w_in, modulate, normed):
    half = other_latent.shape[1]
    normed[:half, :] = own_normed[...]
    normed[half:, :] = shaped(hidden_of(other_latent[...], w_in[...]), 1.0 + modulate[1], modulate[0])


def norm_all(other_latent, own_normed, w_in, modulate):
    half, width = own_normed.shape
    return pl.pallas_call(
        norm_kernel,
        out_shape=jax.ShapeDtypeStruct((2 * half, width), jnp.bfloat16),
        in_specs=[pl.BlockSpec(memory_space=pltpu.VMEM)] * 4,
        out_specs=pl.BlockSpec(memory_space=pltpu.VMEM),
        compiler_params=pltpu.CompilerParams(vmem_limit_bytes=24 * 2**20),
        cost_estimate=pl.CostEstimate(
            flops=2 * half * width * w_in.shape[0], bytes_accessed=6 * half * width, transcendentals=0
        ),
    )(other_latent, own_normed, w_in, modulate)


def attention_kernel(
    normed, first, w_value, w_query, w_key, w_attn_out,
    send, own_mixed, w_out_held, mixed, w_held, sems,
):
    half = normed.shape[0] // 2
    blocks = 1 + w_held.shape[0]
    def fetch(block):
        if block == blocks:
            return [
                pltpu.make_async_copy(w_attn_out.at[rows, :], w_out_held.at[rows, :], sems.at[blocks - 1])
                for place, rows in enumerate(pl.ds(row, PAIR) for row in range(0, w_attn_out.shape[0], PAIR))
            ]
        cols = pl.ds(block * PAIR, PAIR)
        return [
            pltpu.make_async_copy(weight.at[:, cols], w_held.at[block - 1, which], sems.at[block - 1])
            for which, weight in enumerate((w_query, w_key))
        ]

    def arrive(block):
        held = w_out_held if block == blocks else w_held.at[block - 1]
        pltpu.make_async_copy(held, held, sems.at[block - 1]).wait()

    def one(block, which):
        if which == 2:
            weight = w_value[:, block * PAIR : (block + 1) * PAIR]
        else:
            weight = first[which] if block == 0 else w_held[block - 1, which]
        return jnp.dot(normed[...], weight, preferred_element_type=jnp.float32).astype(jnp.bfloat16)

    def project(block):
        return [one(block, which) for which in range(3)]

    for block in range(1, blocks + 1):
        for copy in fetch(block):
            copy.start(priority=int(block > 1))

    ones = jnp.ones((2 * half, HEAD_DIM), jnp.bfloat16)

    def score(query, key, head):
        cols = slice(head * HEAD_DIM, (head + 1) * HEAD_DIM)
        return lax.dot_general(
            query[:, cols], key[:, cols], (((1,), (1,)), ((), ())), preferred_element_type=jnp.float32
        )

    def weigh(scores):
        peak = jnp.max(scores, axis=-1, keepdims=True)
        return jnp.exp2((scores - peak) * (HEAD_DIM ** (-0.5) * LOG2_E)).astype(jnp.bfloat16)

    def mix(block, head, weights, value):
        cols = slice(head * HEAD_DIM, (head + 1) * HEAD_DIM)
        both = jnp.dot(
            weights, jnp.concatenate([value[:, cols], ones], axis=1), preferred_element_type=jnp.float32
        )
        result = (both[:, :HEAD_DIM] / both[:, HEAD_DIM:]).astype(jnp.bfloat16)
        col = block * PAIR + head * HEAD_DIM
        own_mixed[:, col : col + HEAD_DIM] = result[:half]
        mixed[:, col : col + HEAD_DIM] = result[half:]

    def attend(block, query, key, value):
        for head in range(PAIR // HEAD_DIM):
            mix(block, head, weigh(score(query, key, head)), value)

    before = project(0)
    for block in range(1, blocks):
        arrive(block)
        projected = project(block)
        attend(block - 1, *before)
        before = projected
    attend(blocks - 1, *before)
    arrive(blocks)
    for col in range(0, send.shape[1], PAIR):
        cols = slice(col, col + PAIR)
        send[:, cols] = jnp.dot(
            mixed[...], w_out_held[:, cols], preferred_element_type=jnp.float32
        ).astype(jnp.bfloat16)


def attention(normed, first, w_value, w_query, w_key, w_attn_out):
    half = normed.shape[0] // 2
    width, cols = w_query.shape
    blocks = cols // PAIR
    return pl.pallas_call(
        attention_kernel,
        out_shape=(
            jax.ShapeDtypeStruct((half, width), jnp.bfloat16),
            jax.ShapeDtypeStruct((half, cols), jnp.bfloat16),
            jax.ShapeDtypeStruct(w_attn_out.shape, jnp.bfloat16),
        ),
        in_specs=[pl.BlockSpec(memory_space=pltpu.VMEM)] * 3 + [pl.BlockSpec(memory_space=pl.ANY)] * 3,
        out_specs=(pl.BlockSpec(memory_space=pltpu.VMEM),) * 3,
        scratch_shapes=[
            pltpu.VMEM((half, cols), jnp.bfloat16),
            pltpu.VMEM((blocks - 1, 2, width, PAIR), jnp.bfloat16),
            pltpu.SemaphoreType.DMA((blocks,)),
        ],
        compiler_params=pltpu.CompilerParams(vmem_limit_bytes=32 * 2**20),
        cost_estimate=pl.CostEstimate(
            flops=2 * 2 * half * width * cols * 4, bytes_accessed=2 * width * cols * 4, transcendentals=0
        ),
    )(normed, first, w_value, w_query, w_key, w_attn_out)


def own_rows_kernel(own_latent, w_in, modulate, timesteps, chosen, own_mixed, w_attn_out, out, step_size):
    times = jnp.sum(timesteps[...].astype(jnp.float32) * chosen[...], axis=1, keepdims=True)
    step_size[...] = jnp.broadcast_to((times[1:] - times[:1]) / TSCALE, step_size.shape)
    for col in range(0, out.shape[1], PAIR):
        cols = slice(col, col + PAIR)
        partial = jnp.dot(
            own_mixed[...], w_attn_out[:, cols], preferred_element_type=jnp.float32
        ).astype(jnp.bfloat16)
        out[:, cols] = hidden_of(own_latent[...], w_in[:, cols]) + modulate[2, :, cols] * partial.astype(
            jnp.float32
        )


def own_rows(own_latent, w_in, modulate, timesteps, chosen, own_mixed, w_attn_out):
    half, cols = own_mixed.shape
    width = w_attn_out.shape[1]
    return pl.pallas_call(
        own_rows_kernel,
        out_shape=(
            jax.ShapeDtypeStruct((half, width), jnp.float32),
            jax.ShapeDtypeStruct((1, half), jnp.float32),
        ),
        in_specs=[pl.BlockSpec(memory_space=pltpu.VMEM)] * 7,
        out_specs=(pl.BlockSpec(memory_space=pltpu.VMEM),) * 2,
        compiler_params=pltpu.CompilerParams(vmem_limit_bytes=24 * 2**20),
        cost_estimate=pl.CostEstimate(
            flops=2 * half * width * cols, bytes_accessed=4 * half * width, transcendentals=0
        ),
    )(own_latent, w_in, modulate, timesteps, chosen, own_mixed, w_attn_out)


def same(count, key):
    groups = {}
    for step in range(count):
        groups.setdefault(key(*place_of(step)), []).append(step)
    return list(groups.values())


def place_of(step):
    return step % NX, step // NX % NY, step // (NX * NY)


def step_of(x, y, z):
    return (z * NY + y) * NX + x


def prefix_over_steps(term):
    count = lax.axis_size("tm")
    x, y, z = place_of(lax.axis_index("tm"))
    near = jnp.arange(4 * NX, dtype=jnp.int32)
    far = jnp.arange(NY * NZ // 4, dtype=jnp.int32)
    member = step_of(near % NX, y // 2 * 2 + near // NX % 2, z // 2 * 2 + near // (2 * NX))
    target = step_of(x, far % (NY // 2) * 2 + y % 2, far // (NY // 2) * 2 + z % 2)
    wanted = (member[None, :] <= target[:, None]).astype(jnp.bfloat16)
    block = jnp.broadcast_to(term.astype(jnp.bfloat16)[None], near.shape + term.shape)
    block, wanted = lax.optimization_barrier((block, wanted))
    gathered = lax.all_to_all(
        block, "tm", 0, 0, axis_index_groups=same(count, lambda x, y, z: (y // 2, z // 2))
    )
    sums = lax.dot_general(
        wanted, gathered, (((1,), (0,)), ((), ())), preferred_element_type=jnp.float32
    ).astype(jnp.bfloat16)
    parts = lax.all_to_all(
        sums, "tm", 0, 0, axis_index_groups=same(count, lambda x, y, z: (x, y % 2, z % 2))
    )
    return jnp.sum(parts.astype(jnp.float32), axis=0)


def on_device(latents, timesteps, modulation, w_in, w_query, w_key, w_value, w_attn_out, w_final):
    swap = [(0, 1), (1, 0)]
    own_latent = latents[0].T
    other_latent = lax.ppermute(own_latent, "seq", swap)
    modulate = jnp.transpose(modulation, (1, 0, 2))
    there = [
        pltpu.with_memory_space_constraint(array, pltpu.HBM)
        for array in (own_latent, modulate, w_in, timesteps[None], w_query, w_key, w_attn_out)
    ]
    own_normed, first, w_in_held, modulate, own_latent, times = front(*there[:6])
    normed = norm_all(other_latent, own_normed, w_in_held, modulate)
    send, own_mixed, w_out_held = attention(normed, first, w_value, *there[4:])
    received = lax.ppermute(send, "seq", swap)
    ahead = jnp.arange(timesteps.shape[0], dtype=jnp.int32)[None] - lax.axis_index("tm")
    chosen = (ahead == jnp.arange(2, dtype=jnp.int32)[:, None]).astype(jnp.float32)
    own_part, step_size = own_rows(
        own_latent, w_in_held, modulate, times, chosen, own_mixed, w_out_held
    )
    resid = own_part + modulate[2] * received.astype(jnp.float32)
    final = (layer_norm(resid) * (1.0 + modulate[4]) + modulate[3]).astype(jnp.bfloat16)
    drift = lax.dot_general(
        w_final, final, (((0,), (1,)), ((), ())), preferred_element_type=jnp.float32
    )
    return prefix_over_steps(step_size * drift).T[None]


def solution(mesh):
    placed = (
        P("tm", "seq", None),
        P(),
        P("tm", None, None),
        P(),
        P(None, "seq"),
        P(None, "seq"),
        P(None, "seq"),
        P("seq", None),
        P(),
    )
    return jax.shard_map(
        on_device, mesh=mesh, in_specs=placed, out_specs=P("tm", "seq", None), check_vma=False
    )
```

```python
import jax
import jax.numpy as jnp
from jax import lax
from jax.experimental import pallas as pl
from jax.experimental.pallas import tpu as pltpu
from jax.sharding import PartitionSpec as P

HEAD_DIM = 128
PAIR = 2 * HEAD_DIM
LOG2_E = 1.4426950408889634
TSCALE = 1024
NX, NY, NZ = 4, 8, 8

norm_eps = 1e-06


def layer_norm(values):
    center = values - jnp.mean(values, axis=-1, keepdims=True)
    spread = jnp.mean(center * center, axis=-1, keepdims=True)
    return center * lax.rsqrt(spread + norm_eps)


def hidden_of(latent, w_in):
    return lax.dot_general(
        latent.astype(jnp.bfloat16), w_in, (((0,), (0,)), ((), ())), preferred_element_type=jnp.float32
    )


def shaped(hidden, gain, shift):
    return (layer_norm(hidden) * gain + shift).astype(jnp.bfloat16)


def front_kernel(
    own_latent, modulate, w_in, timesteps, w_query, w_key,
    normed, first, w_in_held, modulate_held, latent, timesteps_held, small_sems, sems,
):
    small = [
        pltpu.make_async_copy(own_latent, latent, small_sems.at[0]),
        pltpu.make_async_copy(w_in, w_in_held, small_sems.at[1]),
        pltpu.make_async_copy(modulate, modulate_held, small_sems.at[2]),
        pltpu.make_async_copy(timesteps, timesteps_held, small_sems.at[3]),
    ]
    weights = [
        pltpu.make_async_copy(
            weight.at[:, pl.ds(0, PAIR)], first.at[which], sems.at[which]
        )
        for which, weight in enumerate((w_query, w_key))
    ]
    for copy in small:
        copy.start()
    for copy in weights:
        copy.start(priority=1)
    for copy in small:
        copy.wait()
    normed[...] = shaped(hidden_of(latent[...], w_in_held[...]), 1.0 + modulate_held[1], modulate_held[0])
    for copy in weights:
        copy.wait()


def front(own_latent, modulate, w_in, timesteps, w_query, w_key):
    half = own_latent.shape[1]
    width = w_in.shape[1]
    return pl.pallas_call(
        front_kernel,
        out_shape=(
            jax.ShapeDtypeStruct((half, width), jnp.bfloat16),
            jax.ShapeDtypeStruct((2, width, PAIR), jnp.bfloat16),
            jax.ShapeDtypeStruct(w_in.shape, jnp.bfloat16),
            jax.ShapeDtypeStruct(modulate.shape, jnp.float32),
            jax.ShapeDtypeStruct(own_latent.shape, jnp.float32),
            jax.ShapeDtypeStruct(timesteps.shape, jnp.int32),
        ),
        in_specs=[pl.BlockSpec(memory_space=pl.ANY)] * 6,
        out_specs=(pl.BlockSpec(memory_space=pltpu.VMEM),) * 6,
        scratch_shapes=[
            pltpu.SemaphoreType.DMA((4,)),
            pltpu.SemaphoreType.DMA((2,)),
        ],
        compiler_params=pltpu.CompilerParams(vmem_limit_bytes=24 * 2**20),
        cost_estimate=pl.CostEstimate(
            flops=2 * half * width * w_in.shape[0], bytes_accessed=6 * width * PAIR, transcendentals=0
        ),
    )(own_latent, modulate, w_in, timesteps, w_query, w_key)


def norm_kernel(other_latent, own_normed, w_in, modulate, normed):
    half = other_latent.shape[1]
    normed[:half, :] = own_normed[...]
    normed[half:, :] = shaped(hidden_of(other_latent[...], w_in[...]), 1.0 + modulate[1], modulate[0])


def norm_all(other_latent, own_normed, w_in, modulate):
    half, width = own_normed.shape
    return pl.pallas_call(
        norm_kernel,
        out_shape=jax.ShapeDtypeStruct((2 * half, width), jnp.bfloat16),
        in_specs=[pl.BlockSpec(memory_space=pltpu.VMEM)] * 4,
        out_specs=pl.BlockSpec(memory_space=pltpu.VMEM),
        compiler_params=pltpu.CompilerParams(vmem_limit_bytes=24 * 2**20),
        cost_estimate=pl.CostEstimate(
            flops=2 * half * width * w_in.shape[0], bytes_accessed=6 * half * width, transcendentals=0
        ),
    )(other_latent, own_normed, w_in, modulate)


def attend_head(query, key, value, head):
    cols = slice(head * HEAD_DIM, (head + 1) * HEAD_DIM)
    scores = lax.dot_general(
        query[:, cols], key[:, cols], (((1,), (1,)), ((), ())), preferred_element_type=jnp.float32
    )
    peak = jnp.max(scores, axis=-1, keepdims=True)
    weights = jnp.exp2((scores - peak) * (HEAD_DIM ** (-0.5) * LOG2_E)).astype(jnp.bfloat16)
    ones = jnp.ones((value.shape[0], HEAD_DIM), jnp.bfloat16)
    both = jnp.dot(
        weights, jnp.concatenate([value[:, cols], ones], axis=1), preferred_element_type=jnp.float32
    )
    return (both[:, :HEAD_DIM] / both[:, HEAD_DIM:]).astype(jnp.bfloat16)


def attention_kernel(
    normed, first, w_value, w_query, w_key, w_attn_out,
    send, own_mixed, w_out_held, last_query, last_key, last_value, mixed, w_held, sems,
):
    half = normed.shape[0] // 2
    blocks = 1 + w_held.shape[0]
    def fetch(block):
        if block == blocks:
            return [
                pltpu.make_async_copy(w_attn_out.at[rows, :], w_out_held.at[rows, :], sems.at[blocks - 1])
                for place, rows in enumerate(pl.ds(row, PAIR) for row in range(0, w_attn_out.shape[0], PAIR))
            ]
        cols = pl.ds(block * PAIR, PAIR)
        return [
            pltpu.make_async_copy(weight.at[:, cols], w_held.at[block - 1, which], sems.at[block - 1])
            for which, weight in enumerate((w_query, w_key))
        ]

    def arrive(block):
        held = w_out_held if block == blocks else w_held.at[block - 1]
        pltpu.make_async_copy(held, held, sems.at[block - 1]).wait()

    def one(block, which):
        if which == 2:
            weight = w_value[:, block * PAIR : (block + 1) * PAIR]
        else:
            weight = first[which] if block == 0 else w_held[block - 1, which]
        return jnp.dot(normed[...], weight, preferred_element_type=jnp.float32).astype(jnp.bfloat16)

    def project(block):
        return [one(block, which) for which in range(3)]

    for block in range(1, blocks + 1):
        for copy in fetch(block):
            copy.start(priority=int(block > 1))

    ones = jnp.ones((2 * half, HEAD_DIM), jnp.bfloat16)

    def score(query, key, head):
        cols = slice(head * HEAD_DIM, (head + 1) * HEAD_DIM)
        return lax.dot_general(
            query[:, cols], key[:, cols], (((1,), (1,)), ((), ())), preferred_element_type=jnp.float32
        )

    def weigh(scores):
        peak = jnp.max(scores, axis=-1, keepdims=True)
        return jnp.exp2((scores - peak) * (HEAD_DIM ** (-0.5) * LOG2_E)).astype(jnp.bfloat16)

    def mix(block, head, weights, value):
        cols = slice(head * HEAD_DIM, (head + 1) * HEAD_DIM)
        both = jnp.dot(
            weights, jnp.concatenate([value[:, cols], ones], axis=1), preferred_element_type=jnp.float32
        )
        result = (both[:, :HEAD_DIM] / both[:, HEAD_DIM:]).astype(jnp.bfloat16)
        col = block * PAIR + head * HEAD_DIM
        own_mixed[:, col : col + HEAD_DIM] = result[:half]
        mixed[:, col : col + HEAD_DIM] = result[half:]

    def attend(block, query, key, value):
        for head in range(PAIR // HEAD_DIM):
            mix(block, head, weigh(score(query, key, head)), value)

    before = project(0)
    for block in range(1, blocks):
        arrive(block)
        projected = project(block)
        attend(block - 1, *before)
        before = projected
    query, key, value = before
    last_query[...], last_key[...], last_value[...] = query[:half], key, value
    for head in range(PAIR // HEAD_DIM):
        col = (blocks - 1) * PAIR + head * HEAD_DIM
        mixed[:, col : col + HEAD_DIM] = attend_head(query[half:], key, value, head)
    arrive(blocks)
    for col in range(0, send.shape[1], PAIR):
        cols = slice(col, col + PAIR)
        send[:, cols] = jnp.dot(
            mixed[...], w_out_held[:, cols], preferred_element_type=jnp.float32
        ).astype(jnp.bfloat16)


def attention(normed, first, w_value, w_query, w_key, w_attn_out):
    half = normed.shape[0] // 2
    width, cols = w_query.shape
    blocks = cols // PAIR
    return pl.pallas_call(
        attention_kernel,
        out_shape=(
            jax.ShapeDtypeStruct((half, width), jnp.bfloat16),
            jax.ShapeDtypeStruct((half, cols), jnp.bfloat16),
            jax.ShapeDtypeStruct(w_attn_out.shape, jnp.bfloat16),
            jax.ShapeDtypeStruct((half, PAIR), jnp.bfloat16),
            jax.ShapeDtypeStruct((2 * half, PAIR), jnp.bfloat16),
            jax.ShapeDtypeStruct((2 * half, PAIR), jnp.bfloat16),
        ),
        in_specs=[pl.BlockSpec(memory_space=pltpu.VMEM)] * 3 + [pl.BlockSpec(memory_space=pl.ANY)] * 3,
        out_specs=(pl.BlockSpec(memory_space=pltpu.VMEM),) * 6,
        scratch_shapes=[
            pltpu.VMEM((half, cols), jnp.bfloat16),
            pltpu.VMEM((blocks - 1, 2, width, PAIR), jnp.bfloat16),
            pltpu.SemaphoreType.DMA((blocks,)),
        ],
        compiler_params=pltpu.CompilerParams(vmem_limit_bytes=32 * 2**20),
        cost_estimate=pl.CostEstimate(
            flops=2 * 2 * half * width * cols * 4, bytes_accessed=2 * width * cols * 4, transcendentals=0
        ),
    )(normed, first, w_value, w_query, w_key, w_attn_out)


def own_rows_kernel(own_latent, w_in, modulate, timesteps, chosen, own_mixed, w_attn_out, query, key, value, out, step_size, mixed):
    last = own_mixed.shape[1] - PAIR
    mixed[:, :last] = own_mixed[:, :last]
    for head in range(PAIR // HEAD_DIM):
        col = last + head * HEAD_DIM
        mixed[:, col : col + HEAD_DIM] = attend_head(query[...], key[...], value[...], head)
    times = jnp.sum(timesteps[...].astype(jnp.float32) * chosen[...], axis=1, keepdims=True)
    step_size[...] = jnp.broadcast_to((times[1:] - times[:1]) / TSCALE, step_size.shape)
    for col in range(0, out.shape[1], PAIR):
        cols = slice(col, col + PAIR)
        partial = jnp.dot(
            mixed[...], w_attn_out[:, cols], preferred_element_type=jnp.float32
        ).astype(jnp.bfloat16)
        out[:, cols] = hidden_of(own_latent[...], w_in[:, cols]) + modulate[2, :, cols] * partial.astype(
            jnp.float32
        )


def own_rows(own_latent, w_in, modulate, timesteps, chosen, own_mixed, w_attn_out, *last):
    half, cols = own_mixed.shape
    width = w_attn_out.shape[1]
    return pl.pallas_call(
        own_rows_kernel,
        out_shape=(
            jax.ShapeDtypeStruct((half, width), jnp.float32),
            jax.ShapeDtypeStruct((1, half), jnp.float32),
        ),
        in_specs=[pl.BlockSpec(memory_space=pltpu.VMEM)] * 10,
        out_specs=(pl.BlockSpec(memory_space=pltpu.VMEM),) * 2,
        scratch_shapes=[pltpu.VMEM(own_mixed.shape, jnp.bfloat16)],
        compiler_params=pltpu.CompilerParams(vmem_limit_bytes=24 * 2**20),
        cost_estimate=pl.CostEstimate(
            flops=2 * half * width * cols, bytes_accessed=4 * half * width, transcendentals=0
        ),
    )(own_latent, w_in, modulate, timesteps, chosen, own_mixed, w_attn_out, *last)


def same(count, key):
    groups = {}
    for step in range(count):
        groups.setdefault(key(*place_of(step)), []).append(step)
    return list(groups.values())


def place_of(step):
    return step % NX, step // NX % NY, step // (NX * NY)


def step_of(x, y, z):
    return (z * NY + y) * NX + x


def prefix_over_steps(term):
    count = lax.axis_size("tm")
    x, y, z = place_of(lax.axis_index("tm"))
    near = jnp.arange(4 * NX, dtype=jnp.int32)
    far = jnp.arange(NY * NZ // 4, dtype=jnp.int32)
    member = step_of(near % NX, y // 2 * 2 + near // NX % 2, z // 2 * 2 + near // (2 * NX))
    target = step_of(x, far % (NY // 2) * 2 + y % 2, far // (NY // 2) * 2 + z % 2)
    wanted = (member[None, :] <= target[:, None]).astype(jnp.bfloat16)
    block = jnp.broadcast_to(term.astype(jnp.bfloat16)[None], near.shape + term.shape)
    block, wanted = lax.optimization_barrier((block, wanted))
    gathered = lax.all_to_all(
        block, "tm", 0, 0, axis_index_groups=same(count, lambda x, y, z: (y // 2, z // 2))
    )
    sums = lax.dot_general(
        wanted, gathered, (((1,), (0,)), ((), ())), preferred_element_type=jnp.float32
    ).astype(jnp.bfloat16)
    parts = lax.all_to_all(
        sums, "tm", 0, 0, axis_index_groups=same(count, lambda x, y, z: (x, y % 2, z % 2))
    )
    return jnp.sum(parts.astype(jnp.float32), axis=0)


def on_device(latents, timesteps, modulation, w_in, w_query, w_key, w_value, w_attn_out, w_final):
    swap = [(0, 1), (1, 0)]
    own_latent = latents[0].T
    other_latent = lax.ppermute(own_latent, "seq", swap)
    modulate = jnp.transpose(modulation, (1, 0, 2))
    there = [
        pltpu.with_memory_space_constraint(array, pltpu.HBM)
        for array in (own_latent, modulate, w_in, timesteps[None], w_query, w_key, w_attn_out)
    ]
    own_normed, first, w_in_held, modulate, own_latent, times = front(*there[:6])
    normed = norm_all(other_latent, own_normed, w_in_held, modulate)
    send, own_mixed, w_out_held, *last = attention(normed, first, w_value, *there[4:])
    received = lax.ppermute(send, "seq", swap)
    ahead = jnp.arange(timesteps.shape[0], dtype=jnp.int32)[None] - lax.axis_index("tm")
    chosen = (ahead == jnp.arange(2, dtype=jnp.int32)[:, None]).astype(jnp.float32)
    own_part, step_size = own_rows(
        own_latent, w_in_held, modulate, times, chosen, own_mixed, w_out_held, *last
    )
    resid = own_part + modulate[2] * received.astype(jnp.float32)
    final = (layer_norm(resid) * (1.0 + modulate[4]) + modulate[3]).astype(jnp.bfloat16)
    drift = lax.dot_general(
        w_final, final, (((0,), (1,)), ((), ())), preferred_element_type=jnp.float32
    )
    return prefix_over_steps(step_size * drift).T[None]


def solution(mesh):
    placed = (
        P("tm", "seq", None),
        P(),
        P("tm", None, None),
        P(),
        P(None, "seq"),
        P(None, "seq"),
        P(None, "seq"),
        P("seq", None),
        P(),
    )
    return jax.shard_map(
        on_device, mesh=mesh, in_specs=placed, out_specs=P("tm", "seq", None), check_vma=False
    )
```
